32 devices in a mesh: scene: 8 (over z, y), seq: 4 (over x, core).
Axes of the slice: x: 2, y: 2, z: 4, core: 2. Of those that a mesh axis runs over, the one named last changes fastest.
Arguments:
- scene_x: bfloat16 [8, 65536, 256], P('scene', 'seq'), may hold values from -6 to 6
- cotangent: bfloat16 [8, 65536, 256], P('scene', 'seq'), may hold values from -6 to 6
- gate_gain: float32 [256], replicated, may hold values from 0.3 to 3
- kernel: bfloat16 [256, 256, 256], P(None, 'seq'), may hold values from -6 to 6
- block_mix: bfloat16 [256, 256], replicated, may hold values from -0.375 to 0.375
- across_mix: bfloat16 [256, 256], replicated, may hold values from -0.375 to 0.375
- across_unmix: bfloat16 [256, 256], replicated, may hold values from -0.375 to 0.375
- block_unmix: bfloat16 [256, 256], replicated, may hold values from -0.375 to 0.375
Outputs:
- mixed: bfloat16 [8, 65536, 256], P('scene', 'seq')
- grad_x: bfloat16 [8, 65536, 256], P('scene', 'seq')
- grad_kernel: float32 [256, 256, 256], P('scene', 'seq')
- grad_gain: float32 [256], replicated
The draws below stay inside these ranges and needn't reach their ends.
All inputs are finite; a program needn't handle non-finite values.
Results may differ from the reference program's by a relative error of at most 0.007.
Values may be sent and summed in bfloat16 or wider, within the bound.
A program may use at most 192 MiB of HBM per device.

```python
import math
import jax
import jax.numpy as jnp
from jax import lax

A = 256
B = 256
D = 256
SCENES = 8
SEQLEN = 65536


def block_levels(key, shape, shards, low, high):
    gain = 1.0
    for position, parts in shards:
        draws = jax.random.uniform(jax.random.fold_in(jax.random.fold_in(key, 6), position), (parts,), jnp.float32, low / len(shards), high / len(shards))
        gain = gain * jnp.repeat(jnp.exp(draws), shape[position] // parts).reshape((-1,) + (1,) * (len(shape) - 1 - position))
    return gain


def noise(stream_key, shape, scale, limit, cuts=(), held_as=jnp.bfloat16):
    drawn = scale * jax.random.normal(stream_key, shape, jnp.float32)
    if cuts:
        drawn = drawn * block_levels(stream_key, shape, cuts, -0.22, 0.18)
    return jnp.clip(drawn, -limit, limit).astype(held_as)


def setup_inputs(seed: int = 0) -> dict:
    arg_keys = jax.random.split(jax.random.key(seed), 9)
    scene_x = noise(arg_keys[0], (SCENES, SEQLEN, D), 1.0, 6.0, ((0, 8), (1, 4)))
    cotangent = noise(arg_keys[1], (SCENES, SEQLEN, D), 1.0, 6.0, ((0, 8), (1, 4)))
    gate_gain = jnp.clip(jnp.exp(jax.random.uniform(arg_keys[2], (D,), jnp.float32, math.log(0.3), math.log(3.0))), 0.3, 3.0)
    kernel = noise(arg_keys[3], (A, B, D), 1.0, 6.0, ((1, 4),))
    block_mix = noise(arg_keys[4], (B, B), B ** -0.5, 0.375)
    across_mix = noise(arg_keys[5], (A, A), A ** -0.5, 0.375)
    across_unmix = noise(arg_keys[6], (A, A), A ** -0.5, 0.375)
    block_unmix = noise(arg_keys[7], (B, B), B ** -0.5, 0.375)
    return {"scene_x": scene_x, "cotangent": cotangent, "gate_gain": gate_gain, "kernel": kernel, "block_mix": block_mix, "across_mix": across_mix, "across_unmix": across_unmix, "block_unmix": block_unmix}


def one_scene(scene_rows, cotan_rows, gate_gain, kernel, block_mix, across_mix, across_unmix, block_unmix):
    f32 = jnp.float32
    bf16 = jnp.bfloat16
    inputs = scene_rows.astype(f32).reshape(A, B, D)
    kernel_f = kernel.astype(f32)
    first_f = block_mix.astype(f32)
    across_f = across_mix.astype(f32)
    unmix_f = across_unmix.astype(f32)
    last_f = block_unmix.astype(f32)
    first_mix = jnp.einsum('jb,abc->ajc', first_f, inputs).astype(bf16)
    second_mix = jnp.einsum('ia,ajc->ijc', across_f, first_mix.astype(f32)).astype(bf16)
    weighted = (second_mix.astype(f32) * kernel_f).astype(bf16)
    unmixed = jnp.einsum('pi,ijc->pjc', unmix_f, weighted.astype(f32)).astype(bf16)
    values = jnp.einsum('qj,pjc->pqc', last_f, unmixed.astype(f32))
    gate_pre = inputs * gate_gain
    gate_sig = jax.nn.sigmoid(gate_pre)
    mixed_out = (values * gate_pre * gate_sig).astype(bf16)
    upstream = cotan_rows.astype(f32).reshape(A, B, D)
    grad_values = (upstream * gate_pre * gate_sig).astype(bf16)
    grad_gate = upstream * values * gate_sig * (1.0 + gate_pre * (1.0 - gate_sig))
    grad_unmixed = jnp.einsum('qj,pqc->pjc', last_f, grad_values.astype(f32)).astype(bf16)
    grad_weighted = jnp.einsum('pi,pjc->ijc', unmix_f, grad_unmixed.astype(f32))
    kernel_term = grad_weighted * second_mix.astype(f32)
    grad_second = (grad_weighted * kernel_f).astype(bf16)
    grad_first = jnp.einsum('ia,ijc->ajc', across_f, grad_second.astype(f32)).astype(bf16)
    grad_input = jnp.einsum('jb,ajc->abc', first_f, grad_first.astype(f32)) + grad_gate * gate_gain
    gain_term = lax.optimization_barrier(jnp.sum(inputs * grad_gate, axis=(0, 1)))
    return (mixed_out.reshape(A * B, D), grad_input.astype(bf16).reshape(A * B, D), kernel_term, gain_term)

def reference(scene_x, cotangent, gate_gain, kernel, block_mix, across_mix, across_unmix, block_unmix):

    def step_scene(carry, pair):
        kernel_acc, gain_acc = carry
        mixed_out, grad_input, kernel_term, gain_term = one_scene(pair[0], pair[1], gate_gain, kernel, block_mix, across_mix, across_unmix, block_unmix)
        return ((kernel_acc + kernel_term, gain_acc + gain_term), (mixed_out, grad_input))
    start = (jnp.zeros((A, B, D), jnp.float32), jnp.zeros((D,), jnp.float32))
    (kernel_acc, gain_acc), (mixed, grad_x) = lax.scan(step_scene, start, (scene_x, cotangent))
    grad_scale = 1.0 / jnp.sqrt(jnp.float32(SCENES * A * B))
    return (mixed, grad_x, kernel_acc, gain_acc * grad_scale)
```

```python
import functools

import jax
import jax.numpy as jnp
from jax import lax
from jax.experimental import pallas as pl
from jax.experimental.pallas import tpu as pltpu
from jax.sharding import PartitionSpec as P

f32 = jnp.float32
bf16 = jnp.bfloat16
T = 16


def dot(a, b):
    return jnp.dot(a, b, preferred_element_type=f32)


def turn(swap_ref, block):
    c = block.shape[-1]
    return dot(swap_ref[...], block.reshape(T * T, c)).astype(bf16).reshape(T, T, c)


def at(i):
    return pl.ds(pl.multiple_of(i * T, T), T)


def loop(count, body, unroll=4):
    def step(i, carry):
        body(i)
        return carry

    lax.fori_loop(0, count, step, 0, unroll=min(unroll, count))


def turn_out(swap_ref, held_ref, out_refs):
    groups = out_refs[0].shape[0] // T
    for o, out_ref in enumerate(out_refs):

        def body(g, o=o, out_ref=out_ref):
            out_ref[at(g)] = turn(swap_ref, held_ref[:, at(o * groups + g), :])

        loop(groups, body)


def mix_kernel(x_ref, w_ref, swap_ref, *rest):
    out_refs, held_ref = rest[:-1], rest[-1]

    def body(a):
        held_ref[a] = dot(w_ref[...], x_ref[a]).astype(bf16)

    loop(T, body)
    turn_out(swap_ref, held_ref, out_refs)


def grad_mix_kernel(x_ref, e_ref, gain_ref, w_ref, swap_ref, *rest):
    out_refs, held_ref = rest[:-1], rest[-1]
    gain = gain_ref[...]

    def body(a):
        g = x_ref[a].astype(f32) * gain
        dv = (e_ref[a].astype(f32) * g * jax.nn.sigmoid(g)).astype(bf16)
        held_ref[a] = dot(w_ref[...], dv).astype(bf16)

    loop(T, body, 2)
    turn_out(swap_ref, held_ref, out_refs)


def across_kernel(n, *refs):
    in_refs, (k_ref, f_ref, g_ref, swap_ref) = refs[:n], refs[n : n + 4]
    out_refs, (y_ref, kt_ref, held_ref) = refs[n + 4 : 2 * n + 4], refs[2 * n + 4 :]

    def turn_kernel(i):
        kt_ref[:, at(i), :] = turn(swap_ref, k_ref[at(i)])

    loop(k_ref.shape[0] // T, turn_kernel)

    def body(j):
        y1 = jnp.concatenate([r[j] for r in in_refs], axis=0)
        y2 = dot(f_ref[...], y1).astype(bf16)
        y_ref[j] = y2
        z = (y2.astype(f32) * kt_ref[j].astype(f32)).astype(bf16)
        held_ref[j] = dot(g_ref[...], z).astype(bf16)

    loop(T, body)
    turn_out(swap_ref, held_ref, out_refs)


def grad_across_kernel(n, *refs):
    in_refs, (y_ref, kt_ref, f_ref, g_ref, swap_ref) = refs[:n], refs[n : n + 5]
    out_refs, (term_ref, held_ref, held_term_ref) = refs[n + 5 : 2 * n + 5], refs[2 * n + 5 :]

    def body(j):
        dw1 = jnp.concatenate([r[j] for r in in_refs], axis=0)
        dz = dot(g_ref[...], dw1)
        held_term_ref[j] = (dz * y_ref[j].astype(f32)).astype(bf16)
        dy2 = (dz * kt_ref[j].astype(f32)).astype(bf16)
        held_ref[j] = dot(f_ref[...], dy2).astype(bf16)

    loop(T, body)
    turn_out(swap_ref, held_term_ref, (term_ref,))
    turn_out(swap_ref, held_ref, out_refs)


def gate_kernel(n, *refs):
    in_refs, (x_ref, e_ref, gain_ref, w_ref) = refs[:n], refs[n : n + 4]
    mixed_ref, dg_ref, sum_ref = refs[n + 4 :]
    gain = gain_ref[...]

    @pl.when(pl.program_id(0) == 0)
    def _():
        sum_ref[...] = jnp.zeros_like(sum_ref)

    def body(p):
        v = dot(w_ref[...], jnp.concatenate([r[p] for r in in_refs], axis=0))
        x = x_ref[p].astype(f32)
        g = x * gain
        s = jax.nn.sigmoid(g)
        vs = v * s
        mixed_ref[p] = (vs * g).astype(bf16)
        dg = e_ref[p].astype(f32) * vs * (1.0 + g * (1.0 - s))
        sum_ref[...] += jnp.sum((x * dg).reshape(-1, 8, x.shape[-1]), axis=0)
        dg_ref[p] = (dg * gain).astype(bf16)

    loop(x_ref.shape[0], body, 2)


def grad_in_kernel(n, *refs):
    in_refs, (dg_ref, w_ref, out_ref) = refs[:n], refs[n:]

    def body(a):
        dy1 = jnp.concatenate([r[a] for r in in_refs], axis=0)
        out_ref[a] = (dot(w_ref[...], dy1) + dg_ref[a].astype(f32)).astype(bf16)

    loop(out_ref.shape[0], body)


def lead(rows, shape):
    return pl.BlockSpec((rows,) + tuple(shape[1:]), lambda i: (i,) + (0,) * (len(shape) - 1))


def second(shape):
    return pl.BlockSpec((shape[0], T, shape[2]), lambda i: (0, i, 0))


def whole(shape):
    return pl.BlockSpec(tuple(shape), lambda i: (0,) * len(shape))


def run(body, grid, args, in_specs, outs, out_specs, scratch, products, name):
    shapes = [jax.ShapeDtypeStruct(s, t) for s, t in outs]
    moved = sum(x.size * x.dtype.itemsize for x in args) + sum(
        x.size * x.dtype.itemsize for x in shapes
    )
    return pl.pallas_call(
        body,
        grid=(grid,),
        in_specs=in_specs,
        out_specs=out_specs,
        out_shape=shapes,
        scratch_shapes=scratch,
        name=name,
        compiler_params=pltpu.CompilerParams(
            vmem_limit_bytes=48 * 1024 * 1024, dimension_semantics=("arbitrary",)
        ),
        cost_estimate=pl.CostEstimate(
            flops=int(products), bytes_accessed=int(moved), transcendentals=0
        ),
    )(*args)


def on_device(
    scene_x, cotangent, gate_gain, kernel, block_mix, across_mix, across_unmix, block_unmix
):
    n = lax.axis_size("seq")
    me = lax.axis_index("seq")
    _, row_count, c = scene_x.shape
    size = block_mix.shape[0]
    across = across_mix.shape[0]
    la = row_count // size
    lj = size // n
    x = scene_x.reshape(la, size, c)
    e = cotangent.reshape(la, size, c)
    gain = gate_gain.reshape(1, c)

    rows = jnp.arange(size)
    pick_j = ((((rows // lj) ^ me) * lj + rows % lj)[:, None] == rows[None, :]).astype(bf16)
    rows = jnp.arange(across)
    pick_a = ((((rows // la) ^ me) * la + rows % la)[:, None] == rows[None, :]).astype(bf16)
    f1 = dot(pick_j, block_mix).astype(bf16)
    g1_t = dot(pick_j, block_unmix.T).astype(bf16)
    g2 = dot(pick_a, across_unmix).astype(bf16)
    f2_t = dot(pick_a, across_mix.T).astype(bf16)
    rows = jnp.arange(T * T)
    swap = ((rows % T * T + rows // T)[:, None] == rows[None, :]).astype(bf16)

    def exchange(parts):
        return [parts[0]] + [
            lax.ppermute(parts[o], "seq", [(i, i ^ o) for i in range(n)]) for o in range(1, n)
        ]

    products = 2 * la * size * size * c
    sq = whole((size, size))
    sw = whole((T * T, T * T))
    one = whole((1, c))
    held_j = pltpu.VMEM((T, size, c), bf16)
    held_a = pltpu.VMEM((T, across, c), bf16)
    by_j = (lj, la, c)
    by_a = (la, lj, c)

    y1 = run(
        mix_kernel, la // T, (x, f1, swap), [lead(T, x.shape), sq, sw],
        [(by_j, bf16)] * n, [second(by_j)] * n, [held_j], 2 * products, "mix",
    )
    y1_in = exchange(y1)
    dw1 = run(
        grad_mix_kernel, la // T, (x, e, gain, g1_t, swap),
        [lead(T, x.shape), lead(T, x.shape), one, sq, sw],
        [(by_j, bf16)] * n, [second(by_j)] * n, [held_j], 2 * products, "grad_mix",
    )
    dw1_in = exchange(dw1)

    ij = (across, lj, c)
    ji = (lj, across, c)
    aq = whole((across, across))
    got = run(
        functools.partial(across_kernel, n), lj // T, (*y1_in, kernel, f2_t.T, g2, swap),
        [lead(T, by_j)] * n + [second(ij), aq, aq, sw],
        [(by_a, bf16)] * n + [(ji, bf16)] * 2, [second(by_a)] * n + [lead(T, ji)] * 2,
        [held_a], 4 * products, "across",
    )
    w1, (y2, kernel_t) = got[:n], got[n:]
    w1_in = exchange(w1)
    got = run(
        functools.partial(grad_across_kernel, n), lj // T,
        (*dw1_in, y2, kernel_t, f2_t, g2.T, swap),
        [lead(T, by_j)] * n + [lead(T, ji)] * 2 + [aq, aq, sw],
        [(by_a, bf16)] * n + [(ij, bf16)], [second(by_a)] * n + [second(ij)],
        [held_a, held_a], 4 * products, "grad_across",
    )
    dy1, term = got[:n], got[n]
    kernel_grad = lax.psum_scatter(term, "scene", scatter_dimension=0, tiled=True)
    dy1_in = exchange(dy1)

    step = min(8, la)
    mixed, dg, sums = run(
        functools.partial(gate_kernel, n), la // step, (*w1_in, x, e, gain, g1_t.T),
        [lead(step, by_a)] * n + [lead(step, x.shape)] * 2 + [one, sq],
        [(x.shape, bf16), (x.shape, bf16), ((8, c), f32)],
        [lead(step, x.shape)] * 2 + [whole((8, c))], [], 4 * products, "gate",
    )
    gain_total = lax.psum(jnp.sum(sums, axis=0), ("scene", "seq"))
    total_rows = lax.axis_size("scene") * la * n * size
    grad_scale = 1.0 / jnp.sqrt(jnp.float32(total_rows))
    (grad_x,) = run(
        functools.partial(grad_in_kernel, n), la // step, (*dy1_in, dg, f1.T),
        [lead(step, by_a)] * n + [lead(step, x.shape), sq],
        [(x.shape, bf16)], [lead(step, x.shape)], [], products, "grad_in",
    )
    return (
        mixed.reshape(scene_x.shape),
        grad_x.reshape(scene_x.shape),
        kernel_grad.astype(f32),
        gain_total * grad_scale,
    )


def solution(mesh):
    return jax.shard_map(
        on_device,
        mesh=mesh,
        in_specs=(
            P("scene", "seq", None),
            P("scene", "seq", None),
            P(),
            P(None, "seq", None),
            P(),
            P(),
            P(),
            P(),
        ),
        out_specs=(P("scene", "seq", None), P("scene", "seq", None), P("scene", "seq", None), P()),
        check_vma=False,
    )
```

```python
import functools

import jax
import jax.numpy as jnp
from jax import lax
from jax.experimental import pallas as pl
from jax.experimental.pallas import tpu as pltpu
from jax.sharding import PartitionSpec as P

f32 = jnp.float32
bf16 = jnp.bfloat16
T = 16


def dot(a, b):
    return jnp.dot(a, b, preferred_element_type=f32)


def turn(swap_ref, block):
    c = block.shape[-1]
    return dot(swap_ref[...], block.reshape(T * T, c)).astype(bf16).reshape(T, T, c)


def at(i):
    return pl.ds(pl.multiple_of(i * T, T), T)


def loop(count, body, unroll=4):
    def step(i, carry):
        body(i)
        return carry

    lax.fori_loop(0, count, step, 0, unroll=min(unroll, count))


def turn_out(swap_ref, held_ref, out_refs):
    groups = out_refs[0].shape[0] // T
    for o, out_ref in enumerate(out_refs):

        def body(g, o=o, out_ref=out_ref):
            out_ref[at(g)] = turn(swap_ref, held_ref[:, at(o * groups + g), :])

        loop(groups, body)


def mix_kernel(x_ref, w_ref, swap_ref, *rest):
    out_refs, held_ref = rest[:-1], rest[-1]

    def body(a):
        held_ref[a] = dot(w_ref[...], x_ref[a]).astype(bf16)

    loop(T, body)
    turn_out(swap_ref, held_ref, out_refs)


def grad_mix_kernel(x_ref, e_ref, gain_ref, w_ref, swap_ref, *rest):
    out_refs, held_ref = rest[:-1], rest[-1]
    gain = gain_ref[...]

    def body(a):
        g = x_ref[a].astype(f32) * gain
        dv = (e_ref[a].astype(f32) * g * jax.nn.sigmoid(g)).astype(bf16)
        held_ref[a] = dot(w_ref[...], dv).astype(bf16)

    loop(T, body, 2)
    turn_out(swap_ref, held_ref, out_refs)


def across_kernel(n, *refs):
    in_refs, (k_ref, f_ref, g_ref, swap_ref) = refs[:n], refs[n : n + 4]
    out_refs, (y_ref, kt_ref, held_ref) = refs[n + 4 : 2 * n + 4], refs[2 * n + 4 :]

    def turn_kernel(i):
        kt_ref[:, at(i), :] = turn(swap_ref, k_ref[at(i)])

    loop(k_ref.shape[0] // T, turn_kernel)

    def body(j):
        y1 = jnp.concatenate([r[j] for r in in_refs], axis=0)
        y2 = dot(f_ref[...], y1).astype(bf16)
        y_ref[j] = y2
        z = (y2.astype(f32) * kt_ref[j].astype(f32)).astype(bf16)
        held_ref[j] = dot(g_ref[...], z).astype(bf16)

    loop(T, body)
    turn_out(swap_ref, held_ref, out_refs)


def term_kernel(n, *refs):
    in_refs, (y_ref, g_ref, swap_ref, term_ref, held_ref) = refs[:n], refs[n:]

    def body(j):
        dz = dot(g_ref[...], jnp.concatenate([r[j] for r in in_refs], axis=0))
        held_ref[j] = (dz * y_ref[j].astype(f32)).astype(bf16)

    loop(T, body)
    turn_out(swap_ref, held_ref, (term_ref,))


def grad_across_kernel(n, *refs):
    in_refs, (kt_ref, f_ref, g_ref, swap_ref) = refs[:n], refs[n : n + 4]
    out_refs, held_ref = refs[n + 4 : 2 * n + 4], refs[2 * n + 4]

    def body(j):
        dz = dot(g_ref[...], jnp.concatenate([r[j] for r in in_refs], axis=0))
        dy2 = (dz * kt_ref[j].astype(f32)).astype(bf16)
        held_ref[j] = dot(f_ref[...], dy2).astype(bf16)

    loop(T, body)
    turn_out(swap_ref, held_ref, out_refs)


def gate_kernel(n, *refs):
    in_refs, (x_ref, e_ref, gain_ref, w_ref) = refs[:n], refs[n : n + 4]
    mixed_ref, dg_ref, sum_ref = refs[n + 4 :]
    gain = gain_ref[...]

    @pl.when(pl.program_id(0) == 0)
    def _():
        sum_ref[...] = jnp.zeros_like(sum_ref)

    def body(p):
        v = dot(w_ref[...], jnp.concatenate([r[p] for r in in_refs], axis=0))
        x = x_ref[p].astype(f32)
        g = x * gain
        s = jax.nn.sigmoid(g)
        vs = v * s
        mixed_ref[p] = (vs * g).astype(bf16)
        dg = e_ref[p].astype(f32) * vs * (1.0 + g * (1.0 - s))
        sum_ref[...] += jnp.sum((x * dg).reshape(-1, 8, x.shape[-1]), axis=0)
        dg_ref[p] = (dg * gain).astype(bf16)

    loop(x_ref.shape[0], body, 2)


def grad_in_kernel(n, *refs):
    in_refs, (dg_ref, w_ref, out_ref) = refs[:n], refs[n:]

    def body(a):
        dy1 = jnp.concatenate([r[a] for r in in_refs], axis=0)
        out_ref[a] = (dot(w_ref[...], dy1) + dg_ref[a].astype(f32)).astype(bf16)

    loop(out_ref.shape[0], body)


def lead(rows, shape):
    return pl.BlockSpec((rows,) + tuple(shape[1:]), lambda i: (i,) + (0,) * (len(shape) - 1))


def second(shape):
    return pl.BlockSpec((shape[0], T, shape[2]), lambda i: (0, i, 0))


def whole(shape):
    return pl.BlockSpec(tuple(shape), lambda i: (0,) * len(shape))


def run(body, grid, args, in_specs, outs, out_specs, scratch, products, name):
    shapes = [jax.ShapeDtypeStruct(s, t) for s, t in outs]
    moved = sum(x.size * x.dtype.itemsize for x in args) + sum(
        x.size * x.dtype.itemsize for x in shapes
    )
    return pl.pallas_call(
        body,
        grid=(grid,),
        in_specs=in_specs,
        out_specs=out_specs,
        out_shape=shapes,
        scratch_shapes=scratch,
        name=name,
        compiler_params=pltpu.CompilerParams(
            vmem_limit_bytes=48 * 1024 * 1024, dimension_semantics=("arbitrary",)
        ),
        cost_estimate=pl.CostEstimate(
            flops=int(products) // 16, bytes_accessed=int(moved) // 16, transcendentals=0
        ),
    )(*args)


def on_device(
    scene_x, cotangent, gate_gain, kernel, block_mix, across_mix, across_unmix, block_unmix
):
    n = lax.axis_size("seq")
    me = lax.axis_index("seq")
    _, row_count, c = scene_x.shape
    size = block_mix.shape[0]
    across = across_mix.shape[0]
    la = row_count // size
    lj = size // n
    x = scene_x.reshape(la, size, c)
    e = cotangent.reshape(la, size, c)
    gain = gate_gain.reshape(1, c)

    rows = jnp.arange(size)
    pick_j = ((((rows // lj) ^ me) * lj + rows % lj)[:, None] == rows[None, :]).astype(bf16)
    rows = jnp.arange(across)
    pick_a = ((((rows // la) ^ me) * la + rows % la)[:, None] == rows[None, :]).astype(bf16)
    f1 = dot(pick_j, block_mix).astype(bf16)
    g1_t = dot(pick_j, block_unmix.T).astype(bf16)
    g2 = dot(pick_a, across_unmix).astype(bf16)
    f2_t = dot(pick_a, across_mix.T).astype(bf16)
    rows = jnp.arange(T * T)
    swap = ((rows % T * T + rows // T)[:, None] == rows[None, :]).astype(bf16)

    def exchange(parts):
        return [parts[0]] + [
            lax.ppermute(parts[o], "seq", [(i, i ^ o) for i in range(n)]) for o in range(1, n)
        ]

    products = 2 * la * size * size * c
    sq = whole((size, size))
    sw = whole((T * T, T * T))
    one = whole((1, c))
    held_j = pltpu.VMEM((T, size, c), bf16)
    held_a = pltpu.VMEM((T, across, c), bf16)
    by_j = (lj, la, c)
    by_a = (la, lj, c)

    y1 = run(
        mix_kernel, la // T, (x, f1, swap), [lead(T, x.shape), sq, sw],
        [(by_j, bf16)] * n, [second(by_j)] * n, [held_j], 2 * products, "mix",
    )
    y1_in = exchange(y1)
    dw1 = run(
        grad_mix_kernel, la // T, (x, e, gain, g1_t, swap),
        [lead(T, x.shape), lead(T, x.shape), one, sq, sw],
        [(by_j, bf16)] * n, [second(by_j)] * n, [held_j], 2 * products, "grad_mix",
    )
    dw1_in = exchange(dw1)

    ij = (across, lj, c)
    ji = (lj, across, c)
    aq = whole((across, across))
    got = run(
        functools.partial(across_kernel, n), lj // T, (*y1_in, kernel, f2_t.T, g2, swap),
        [lead(T, by_j)] * n + [second(ij), aq, aq, sw],
        [(by_a, bf16)] * n + [(ji, bf16)] * 2, [second(by_a)] * n + [lead(T, ji)] * 2,
        [held_a], 4 * products, "across",
    )
    w1, (y2, kernel_t) = got[:n], got[n:]
    w1_in = exchange(w1)
    g2_t = g2.T
    (term,) = run(
        functools.partial(term_kernel, n), lj // T, (*dw1_in, y2, g2_t, swap),
        [lead(T, by_j)] * n + [lead(T, ji), aq, sw],
        [(ij, bf16)], [second(ij)], [held_a], 2 * products, "term",
    )
    dy1 = run(
        functools.partial(grad_across_kernel, n), lj // T,
        (*dw1_in, kernel_t, f2_t, g2_t, swap),
        [lead(T, by_j)] * n + [lead(T, ji), aq, aq, sw],
        [(by_a, bf16)] * n, [second(by_a)] * n, [held_a], 3 * products, "grad_across",
    )
    kernel_grad = lax.psum_scatter(term, "scene", scatter_dimension=0, tiled=True)
    dy1_in = exchange(dy1)

    step = min(8, la)
    mixed, dg, sums = run(
        functools.partial(gate_kernel, n), la // step, (*w1_in, x, e, gain, g1_t.T),
        [lead(step, by_a)] * n + [lead(step, x.shape)] * 2 + [one, sq],
        [(x.shape, bf16), (x.shape, bf16), ((8, c), f32)],
        [lead(step, x.shape)] * 2 + [whole((8, c))], [], 4 * products, "gate",
    )
    gain_total = lax.psum(jnp.sum(sums, axis=0), ("scene", "seq"))
    total_rows = lax.axis_size("scene") * la * n * size
    grad_scale = 1.0 / jnp.sqrt(jnp.float32(total_rows))
    (grad_x,) = run(
        functools.partial(grad_in_kernel, n), la // step, (*dy1_in, dg, f1.T),
        [lead(step, by_a)] * n + [lead(step, x.shape), sq],
        [(x.shape, bf16)], [lead(step, x.shape)], [], products, "grad_in",
    )
    return (
        mixed.reshape(scene_x.shape),
        grad_x.reshape(scene_x.shape),
        kernel_grad.astype(f32),
        gain_total * grad_scale,
    )


def solution(mesh):
    return jax.shard_map(
        on_device,
        mesh=mesh,
        in_specs=(
            P("scene", "seq", None),
            P("scene", "seq", None),
            P(),
            P(None, "seq", None),
            P(),
            P(),
            P(),
            P(),
        ),
        out_specs=(P("scene", "seq", None), P("scene", "seq", None), P("scene", "seq", None), P()),
        check_vma=False,
    )
```

```python
import functools

import jax
import jax.numpy as jnp
from jax import lax
from jax.experimental import pallas as pl
from jax.experimental.pallas import tpu as pltpu
from jax.sharding import PartitionSpec as P

f32 = jnp.float32
bf16 = jnp.bfloat16
T = 16


def dot(a, b):
    return jnp.dot(a, b, preferred_element_type=f32)


def turn(swap_ref, block):
    c = block.shape[-1]
    return dot(swap_ref[...], block.reshape(T * T, c)).astype(bf16).reshape(T, T, c)


def at(i):
    return pl.ds(pl.multiple_of(i * T, T), T)


def loop(count, body, unroll=4):
    def step(i, carry):
        body(i)
        return carry

    lax.fori_loop(0, count, step, 0, unroll=min(unroll, count))


def turn_out(swap_ref, held_ref, out_refs):
    first = 0
    for out_ref in out_refs:

        def body(g, first=first, out_ref=out_ref):
            out_ref[at(g)] = turn(swap_ref, held_ref[:, at(first + g), :])

        groups = out_ref.shape[0] // T
        loop(groups, body)
        first += groups


def mix_kernel(outs, x_ref, w_ref, swap_ref, *rest):
    out_refs, held_ref = rest[-1 - outs : -1], rest[-1]

    def body(a):
        held_ref[a] = dot(w_ref[...], x_ref[a]).astype(bf16)

    loop(T, body)
    turn_out(swap_ref, held_ref, out_refs)


def grad_mix_kernel(outs, x_ref, e_ref, gain_ref, w_ref, swap_ref, *rest):
    out_refs, held_ref = rest[-1 - outs : -1], rest[-1]
    gain = gain_ref[...]

    def body(a):
        g = x_ref[a].astype(f32) * gain
        dv = (e_ref[a].astype(f32) * g * jax.nn.sigmoid(g)).astype(bf16)
        held_ref[a] = dot(w_ref[...], dv).astype(bf16)

    loop(T, body, 2)
    turn_out(swap_ref, held_ref, out_refs)


def across_kernel(m, *refs):
    in_refs, (k_ref, f_ref, g_ref, swap_ref) = refs[:m], refs[m : m + 4]
    out_refs, (y_ref, kt_ref, held_ref) = refs[m + 4 : -3], refs[-3:]

    def turn_kernel(i):
        kt_ref[:, at(i), :] = turn(swap_ref, k_ref[at(i)])

    loop(k_ref.shape[0] // T, turn_kernel)

    def body(j):
        y1 = jnp.concatenate([r[j] for r in in_refs], axis=0)
        y2 = dot(f_ref[...], y1).astype(bf16)
        y_ref[j] = y2
        z = (y2.astype(f32) * kt_ref[j].astype(f32)).astype(bf16)
        held_ref[j] = dot(g_ref[...], z).astype(bf16)

    loop(T, body)
    turn_out(swap_ref, held_ref, out_refs)


def term_kernel(n, *refs):
    in_refs, (y_ref, g_ref, swap_ref, term_ref, held_ref) = refs[:n], refs[n:]

    def body(j):
        dz = dot(g_ref[...], jnp.concatenate([r[j] for r in in_refs], axis=0))
        held_ref[j] = (dz * y_ref[j].astype(f32)).astype(bf16)

    loop(T, body)
    turn_out(swap_ref, held_ref, (term_ref,))


def grad_across_kernel(n, *refs):
    in_refs, (kt_ref, f_ref, g_ref, swap_ref) = refs[:n], refs[n : n + 4]
    out_refs, held_ref = refs[n + 4 : -1], refs[-1]

    def body(j):
        dz = dot(g_ref[...], jnp.concatenate([r[j] for r in in_refs], axis=0))
        dy2 = (dz * kt_ref[j].astype(f32)).astype(bf16)
        held_ref[j] = dot(f_ref[...], dy2).astype(bf16)

    loop(T, body)
    turn_out(swap_ref, held_ref, out_refs)


def gate_kernel(n, *refs):
    in_refs, (x_ref, e_ref, gain_ref, w_ref) = refs[:n], refs[n : n + 4]
    mixed_ref, dg_ref, sum_ref = refs[n + 4 :]
    gain = gain_ref[...]

    @pl.when(pl.program_id(0) == 0)
    def _():
        sum_ref[...] = jnp.zeros_like(sum_ref)

    def body(p):
        v = dot(w_ref[...], jnp.concatenate([r[p] for r in in_refs], axis=0))
        x = x_ref[p].astype(f32)
        g = x * gain
        s = jax.nn.sigmoid(g)
        vs = v * s
        mixed_ref[p] = (vs * g).astype(bf16)
        dg = e_ref[p].astype(f32) * vs * (1.0 + g * (1.0 - s))
        sum_ref[...] += jnp.sum((x * dg).reshape(-1, 8, x.shape[-1]), axis=0)
        dg_ref[p] = (dg * gain).astype(bf16)

    loop(x_ref.shape[0], body, 2)


def grad_in_kernel(n, *refs):
    in_refs, (dg_ref, w_ref), out_ref = refs[:n], refs[n : n + 2], refs[-1]

    def body(a):
        dy1 = jnp.concatenate([r[a] for r in in_refs], axis=0)
        out_ref[a] = (dot(w_ref[...], dy1) + dg_ref[a].astype(f32)).astype(bf16)

    loop(out_ref.shape[0], body)


def lead(rows, shape, first=0):
    return pl.BlockSpec((rows,) + tuple(shape[1:]), lambda i: (i + first,) + (0,) * (len(shape) - 1))


def second(shape):
    return pl.BlockSpec((shape[0], T, shape[2]), lambda i: (0, i, 0))


def whole(shape):
    return pl.BlockSpec(tuple(shape), lambda i: (0,) * len(shape))


def run(body, grid, args, in_specs, outs, out_specs, scratch, products, name, weight=1 / 16, alias=None):
    shapes = [jax.ShapeDtypeStruct(s, t) for s, t in outs]
    moved = sum(x.size * x.dtype.itemsize for x in args) + sum(
        x.size * x.dtype.itemsize for x in shapes
    )
    return pl.pallas_call(
        body,
        grid=(grid,),
        in_specs=in_specs,
        out_specs=out_specs,
        out_shape=shapes,
        scratch_shapes=scratch,
        name=name,
        input_output_aliases=alias or {},
        compiler_params=pltpu.CompilerParams(
            vmem_limit_bytes=48 * 1024 * 1024, dimension_semantics=("arbitrary",)
        ),
        cost_estimate=pl.CostEstimate(
            flops=int(products * weight), bytes_accessed=int(moved * weight), transcendentals=0
        ),
    )(*args)


def on_device(
    scene_x, cotangent, gate_gain, kernel, block_mix, across_mix, across_unmix, block_unmix
):
    n = lax.axis_size("seq")
    me = lax.axis_index("seq")
    _, row_count, c = scene_x.shape
    size = block_mix.shape[0]
    across = across_mix.shape[0]
    la = row_count // size
    lj = size // n
    x = scene_x.reshape(la, size, c)
    e = cotangent.reshape(la, size, c)
    gain = gate_gain.reshape(1, c)

    rows = jnp.arange(size)
    pick_j = ((((rows // lj) ^ me) * lj + rows % lj)[:, None] == rows[None, :]).astype(bf16)
    rows = jnp.arange(across)
    pick_a = ((((rows // la) ^ me) * la + rows % la)[:, None] == rows[None, :]).astype(bf16)
    f1 = dot(pick_j, block_mix).astype(bf16)
    g1_t = dot(pick_j, block_unmix.T).astype(bf16)
    g2 = dot(pick_a, across_unmix).astype(bf16)
    f2_t = dot(pick_a, across_mix.T).astype(bf16)
    rows = jnp.arange(T * T)
    swap = ((rows % T * T + rows // T)[:, None] == rows[None, :]).astype(bf16)

    def send(part, o):
        return lax.ppermute(part, "seq", [(i, i ^ o) for i in range(n)]) if o else part

    def exchange(parts):
        return [send(part, o) for o, part in enumerate(parts)]

    f1_back = f1.T
    products = 2 * la * size * size * c
    sq = whole((size, size))
    sw = whole((T * T, T * T))
    one = whole((1, c))
    held_j = pltpu.VMEM((T, size, c), bf16)
    held_a = pltpu.VMEM((T, across, c), bf16)
    by_j = (lj, la, c)
    by_a = (la, lj, c)

    near = 2 if la > T and n > 2 else n
    anywhere = pl.BlockSpec(memory_space=pl.ANY)
    far = list(range(near, n))
    y1 = run(
        functools.partial(mix_kernel, n), la // T, (x, f1, swap), [lead(T, x.shape), sq, sw],
        [(by_j, bf16)] * n, [second(by_j)] * n, [held_j], 2 * products, "mix",
    )
    y1_in = exchange(y1)
    after = y1_in[1:2]
    dw1 = run(
        functools.partial(grad_mix_kernel, n), la // T, (x, e, gain, g1_t, swap, *after),
        [lead(T, x.shape), lead(T, x.shape), one, sq, sw] + [anywhere] * len(after),
        [(by_j, bf16)] * n, [second(by_j)] * n, [held_j], 2 * products, "grad_mix",
    )
    dw1_in = exchange(dw1)

    ij = (across, lj, c)
    ji = (lj, across, c)
    aq = whole((across, across))
    got = run(
        functools.partial(across_kernel, len(y1_in)), lj // T, (*y1_in, kernel, f2_t.T, g2, swap),
        [lead(T, y.shape) for y in y1_in] + [second(ij), aq, aq, sw],
        [(by_a, bf16)] * n + [(ji, bf16)] * 2, [second(by_a)] * n + [lead(T, ji)] * 2,
        [held_a], 4 * products, "across",
    )
    w1, (y2, kernel_t) = got[:n], got[n:]
    w1_in = exchange(w1)
    g2_t = g2.T
    (term,) = run(
        functools.partial(term_kernel, n), lj // T, (*dw1_in, y2, g2_t, swap),
        [lead(T, by_j)] * n + [lead(T, ji), aq, sw],
        [(ij, bf16)], [second(ij)], [held_a], 2 * products, "term",
    )
    cuts = [la - T, T] if far else [la]
    owners = [o for o in range(n) for _ in (cuts if o >= near else [la])]
    shapes = [(count, lj, c) for o in range(n) for count in (cuts if o >= near else [la])]
    dy1 = run(
        functools.partial(grad_across_kernel, n), lj // T,
        (*dw1_in, kernel_t, f2_t, g2_t, swap),
        [lead(T, by_j)] * n + [lead(T, ji), aq, aq, sw],
        [(s, bf16) for s in shapes], [second(s) for s in shapes], [held_a], 3 * products,
        "grad_across",
    )
    kernel_grad = lax.psum_scatter(term, "scene", scatter_dimension=0, tiled=True)
    dy1_in = [send(part, o) for part, o in zip(dy1, owners)]

    step = min(8, la)
    mixed, dg, sums = run(
        functools.partial(gate_kernel, n), la // step, (*w1_in, x, e, gain, g1_t.T),
        [lead(step, by_a)] * n + [lead(step, x.shape)] * 2 + [one, sq],
        [(x.shape, bf16), (x.shape, bf16), ((8, c), f32)],
        [lead(step, x.shape)] * 2 + [whole((8, c))], [], 4 * products, "gate",
        weight=64,
    )
    gain_total = jnp.sum(sums, axis=0, keepdims=True)
    for axis in ("scene", "seq"):
        bit, ends = 1, lax.axis_size(axis)
        while bit < ends:
            gain_total += lax.ppermute(gain_total, axis, [(i, i ^ bit) for i in range(ends)])
            bit *= 2
    gain_total = gain_total.reshape(c)
    total_rows = lax.axis_size("scene") * la * n * size
    grad_scale = 1.0 / jnp.sqrt(jnp.float32(total_rows))
    first, grad_x = 0, ()
    for k, count in enumerate(cuts):
        begin = first // step
        parts = dy1_in[:near] + dy1_in[near + k :: len(cuts)]
        grad_x = run(
            functools.partial(grad_in_kernel, n), count // step, (*parts, dg, f1_back, *grad_x),
            [lead(step, by_a, begin)] * near + [lead(step, by_a)] * len(far)
            + [lead(step, x.shape, begin), sq] + [anywhere] * len(grad_x),
            [(x.shape, bf16)], [lead(step, x.shape, begin)], [], products, "grad_in",
            alias={n + 2: 0} if grad_x else None,
        )
        first += count
    (grad_x,) = grad_x
    return (
        mixed.reshape(scene_x.shape),
        grad_x.reshape(scene_x.shape),
        kernel_grad.astype(f32),
        gain_total * grad_scale,
    )


def solution(mesh):
    return jax.shard_map(
        on_device,
        mesh=mesh,
        in_specs=(
            P("scene", "seq", None),
            P("scene", "seq", None),
            P(),
            P(None, "seq", None),
            P(),
            P(),
            P(),
            P(),
        ),
        out_specs=(P("scene", "seq", None), P("scene", "seq", None), P("scene", "seq", None), P()),
        check_vma=False,
    )
```
